32 devices in a mesh: dp: 8 (over z, x), seq: 2 (over core), sect: 2 (over y).
Axes of the slice: x: 2, y: 2, z: 4, core: 2. Of those that a mesh axis runs over, the one named last changes fastest.
Arguments:
- bases: int32 [16, 512], P(('dp', 'sect'), 'seq'), may hold values from 0 to 3
- embed: bfloat16 [5, 4, 384], replicated, may hold values from -2.5 to 2.5
- conv_w: bfloat16 [5, 384, 384], P(None, 'seq'), may hold values from -0.125 to 0.125
- w_in: bfloat16 [384, 768], P('seq', 'sect'), may hold values from -0.3125 to 0.3125
- w_out: bfloat16 [768, 384], P('sect', 'seq'), may hold values from -0.21875 to 0.21875
- cotangent: bfloat16 [16, 512, 384], P(('dp', 'sect'), 'seq'), may hold values from -0.15625 to 0.15625
Outputs:
- output: bfloat16 [16, 512, 384], P(('dp', 'sect'), 'seq')
- grad_embed: float32 [5, 4, 384], P(None, None, 'seq')
- grad_conv: float32 [5, 384, 384], P(None, 'seq')
- grad_in: float32 [384, 768], P('seq', 'sect')
- grad_out: float32 [768, 384], P('sect', 'seq')
The draws below stay inside these ranges and needn't reach their ends.
All inputs are finite; a program needn't handle non-finite values.
Results may differ from the reference program's by a relative error of at most 0.0088.
Values may be sent and summed in bfloat16 or wider, within the bound.
A program may use at most 64 MiB of HBM per device.

```python
import jax
import jax.numpy as jnp
from jax import lax

C = 384
F = 768
TAPS = 5
BASES = 4
LENGTH = 512
SAMPLES = 16


def set_ends(result, stream_key, smallest, largest):
    extent = result.shape
    place = [jax.random.randint(jax.random.fold_in(stream_key, axis), (), 0, extent[axis]) for axis in range(len(extent))]
    result = result.at[tuple(place)].set(smallest)
    longest = extent.index(max(extent))
    place[longest] = (place[longest] + 1) % extent[longest]
    return result.at[tuple(place)].set(largest)


def block_scale(key, shape, cuts, least, high):
    def one(position, parts):
        steps = jax.random.uniform(jax.random.fold_in(jax.random.fold_in(key, 6), position), (parts,), jnp.float32, least / len(cuts), high / len(cuts))
        return jnp.repeat(jnp.exp(steps), shape[position] // parts).reshape((-1,) + (1,) * (len(shape) - position - 1))

    level = one(*cuts[0])
    for cut in cuts[1:]:
        level = level * one(*cut)
    return level


def noise(rng, dims, width, limit, shards=(), kind=jnp.bfloat16):
    level = block_scale(rng, dims, shards, -0.22, 0.18) if shards else 1.0
    drawn = jax.random.normal(rng, dims, jnp.float32) * width * level
    return jnp.minimum(jnp.maximum(drawn, -limit), limit).astype(kind)


def setup_inputs(seed: int = 0) -> dict:
    key_list = jax.random.split(jax.random.key(seed), 7)
    bases = set_ends(jax.random.randint(key_list[0], (SAMPLES, LENGTH), 0, 4), jax.random.fold_in(key_list[0], 1), 0, 3).astype(jnp.int32)
    embed = noise(key_list[1], (TAPS, BASES, C), TAPS ** -0.5, 2.5)
    conv_w = noise(key_list[2], (TAPS, C, C), (TAPS * C) ** -0.5, 0.125, ((1, 2),))
    w_in = noise(key_list[3], (C, F), C ** -0.5, 0.3125, ((0, 2), (1, 2)))
    w_out = noise(key_list[4], (F, C), F ** -0.5, 0.21875, ((0, 2), (1, 2)))
    cotangent = noise(key_list[5], (SAMPLES, LENGTH, C), (1.0 / (LENGTH * SAMPLES) ** 0.5), 0.15625, ((0, 16), (1, 2)))
    return dict(bases=bases, embed=embed, conv_w=conv_w, w_in=w_in, w_out=w_out, cotangent=cotangent)


def gelu_tanh(value):
    return jax.nn.gelu(value, approximate=True)

def gelu_back(value, grad):
    unused, pull = jax.vjp(gelu_tanh, value)
    return pull(grad)[0]

def contract_rows(left, right):
    return lax.dot_general(left, right, (((0,), (0,)), ((), ())), preferred_element_type=jnp.float32)

def contract_cols(left, right):
    return lax.dot_general(left, right, (((1,), (1,)), ((), ())), preferred_element_type=jnp.float32)

def one_sample(ids, embed, conv_w, w_in, w_out, cot):
    rows = ids.shape[0]
    chans = embed.shape[2]
    padded_ids = jnp.pad(ids + 1, 2)
    levels = jnp.arange(1, BASES + 1, dtype=jnp.int32)
    onehots = [(padded_ids[k:k + rows, None] == levels[None, :]).astype(jnp.bfloat16) for k in range(TAPS)]
    accum = jnp.zeros((rows, chans), jnp.float32)
    for k in range(TAPS):
        accum = accum + jnp.dot(onehots[k], embed[k], preferred_element_type=jnp.float32)
    h_zero = accum.astype(jnp.bfloat16)
    h_padded = jnp.pad(h_zero, ((2, 2), (0, 0)))
    pre_conv = jnp.zeros((rows, chans), jnp.float32)
    for k in range(TAPS):
        pre_conv = pre_conv + jnp.dot(h_padded[k:k + rows], conv_w[k], preferred_element_type=jnp.float32)
    h_one = lax.optimization_barrier((h_zero.astype(jnp.float32) + gelu_tanh(pre_conv)).astype(jnp.bfloat16))
    h_onef = h_one.astype(jnp.float32)
    pooled = lax.optimization_barrier((h_onef.reshape(rows // 2, 2, chans).sum(1) * 0.5).astype(jnp.bfloat16))
    pooledf = pooled.astype(jnp.float32)
    scale = lax.rsqrt(lax.optimization_barrier(jnp.mean(pooledf * pooledf, axis=-1, keepdims=True)) + 1e-06)
    normed = (pooledf * scale).astype(jnp.bfloat16)
    pre = jnp.dot(normed, w_in, preferred_element_type=jnp.float32)
    act = gelu_tanh(pre).astype(jnp.bfloat16)
    mixed = lax.optimization_barrier(jnp.dot(act, w_out, preferred_element_type=jnp.float32).astype(jnp.bfloat16))
    output = (h_onef + jnp.repeat(mixed.astype(jnp.float32), 2, axis=0)).astype(jnp.bfloat16)
    dout = cot.astype(jnp.float32)
    dmixed = dout.reshape(rows // 2, 2, chans).sum(1).astype(jnp.bfloat16)
    grad_out = contract_rows(act, dmixed)
    dact = contract_cols(dmixed, w_out)
    dpre = gelu_back(pre, dact).astype(jnp.bfloat16)
    grad_in = contract_rows(normed, dpre)
    dnormed = contract_cols(dpre, w_in)
    dpooled = scale * dnormed - pooledf * scale ** 3 * lax.optimization_barrier(jnp.mean(dnormed * pooledf, axis=-1, keepdims=True))
    dh_one = dout + jnp.repeat(dpooled * 0.5, 2, axis=0)
    dz_rows = gelu_back(pre_conv, dh_one).astype(jnp.bfloat16)
    dz_padded = jnp.pad(dz_rows, ((2, 2), (0, 0)))
    dh_zero = dh_one
    for k in range(TAPS):
        dh_zero = dh_zero + contract_cols(dz_padded[4 - k:4 - k + rows], conv_w[k])
    grad_conv = jnp.stack([contract_rows(h_padded[k:k + rows], dz_rows) for k in range(TAPS)])
    grad_embed = jnp.stack([lax.dot_general(onehots[k].astype(jnp.float32), dh_zero, (((0,), (0,)), ((), ())), precision=lax.Precision.HIGHEST, preferred_element_type=jnp.float32) for k in range(TAPS)])
    return (output, grad_embed, grad_conv, grad_in, grad_out)

def reference(bases, embed, conv_w, w_in, w_out, cotangent):

    def stepper(carry, item):
        ids, cot = item
        output, g_embed, g_conv, g_in, g_out = one_sample(ids, embed, conv_w, w_in, w_out, cot)
        carry = (carry[0] + g_embed, carry[1] + g_conv, carry[2] + g_in, carry[3] + g_out)
        return (carry, output)
    start = (jnp.zeros(embed.shape, jnp.float32), jnp.zeros(conv_w.shape, jnp.float32), jnp.zeros(w_in.shape, jnp.float32), jnp.zeros(w_out.shape, jnp.float32))
    totals, outputs = lax.scan(stepper, start, (bases, cotangent))
    return (outputs, totals[0], totals[1], totals[2], totals[3])
```

```python
import functools

import jax
import jax.numpy as jnp
from jax import lax
from jax.experimental import pallas as pl
from jax.experimental.pallas import tpu as pltpu
from jax.sharding import PartitionSpec as P

TAPS = 5
BASES = 4


def swapped(value, axis, apart):
    mask = 2**apart
    pairs = [(source, source ^ mask) for source in range(lax.axis_size(axis))]
    return lax.ppermute(value, axis, pairs)


def padded(cells, sides, width):
    for axis, dim in sides:
        count = lax.axis_size(axis)
        ends = count - 1
        head = lax.slice_in_dim(cells, 0, width, axis=dim)
        tail = lax.slice_in_dim(cells, cells.shape[dim] - width, cells.shape[dim], axis=dim)
        cells = jnp.concatenate(
            [
                lax.ppermute(tail, axis, [(i, (i + 1) % count) for i in range(ends)]),
                cells,
                lax.ppermute(head, axis, [((i + 1) % count, i) for i in range(ends)]),
            ],
            axis=dim,
        )
    return cells


def gelu_tanh(value):
    return jax.nn.gelu(value, approximate=True)


def gelu_back(value, grad):
    unused, pull = jax.vjp(gelu_tanh, value)
    return pull(grad)[0]


def contract_rows(left, right):
    return lax.dot_general(
        left, right, (((0,), (0,)), ((), ())), preferred_element_type=jnp.float32
    )


def contract_cols(left, right):
    return lax.dot_general(
        left, right, (((1,), (1,)), ((), ())), preferred_element_type=jnp.float32
    )


def partner_rows(value):
    return swapped(value, "sect", 0)


def partner_sums(value):
    return swapped(value.astype(jnp.bfloat16), "sect", 0).astype(value.dtype)


def remote(src, dst, send, recv, place):
    return pltpu.make_async_remote_copy(
        src_ref=src,
        dst_ref=dst,
        send_sem=send,
        recv_sem=recv,
        device_id=place,
        device_id_type=pl.DeviceIdType.MESH,
    )


def reduce_kernel(
    seqs, high, conv_in, feed_in, conv_out, feed_out,
    conv_r0, feed_r0, conv_a1, feed_a1, conv_r1, feed_r1, conv_a2, feed_a2,
    conv_r2, feed_r2, conv_all, feed_all,
    s0, r0, s1, r1, s2, r2, s3, r3, s4, r4,
):
    me_seq = lax.axis_index("seq")
    me_sect = lax.axis_index("sect")
    me_dp = lax.axis_index("dp")
    low = lax.rem(me_dp, 2)
    up = me_dp // 2
    quad = me_sect * 2 + low
    conv_block, feed_block = conv_a2.shape[0], feed_a2.shape[0]
    conv_piece, feed_piece = conv_r2.shape[1], feed_r2.shape[1]

    seq_ids = [lax.rem(me_seq + k, seqs) for k in range(1, seqs)]
    quad_ids = [(k // 2, k % 2) for k in range(1, 4)]
    quad_ids = [
        (lax.rem(me_sect + a, 2), lax.rem(low + b, 2)) for a, b in quad_ids
    ]
    high_ids = [lax.rem(up + k, high) for k in range(1, high)]
    seq_place = [{"seq": p} for p in seq_ids]
    quad_place = [{"sect": a, "dp": up * 2 + b} for a, b in quad_ids]
    high_place = [{"dp": p * 2 + low} for p in high_ids]

    barrier = pltpu.get_barrier_semaphore()
    for place in seq_place + quad_place + high_place:
        pl.semaphore_signal(
            barrier, inc=1, device_id=place, device_id_type=pl.DeviceIdType.MESH
        )
    pl.semaphore_wait(barrier, len(seq_place) + len(quad_place) + len(high_place))

    def rows(index, size):
        return pl.ds(pl.multiple_of(index * size, size), size)

    def finish(copies):
        for copy in copies:
            copy.wait_recv()
        for copy in copies:
            copy.wait_send()

    def total(count, size, dest, own, slots):
        def body(i, carry):
            at = rows(i, size)
            value = own(at).astype(jnp.float32)
            for slot in range(slots.shape[0]):
                value = value + slots[slot, at].astype(jnp.float32)
            dest[at] = value.astype(dest.dtype)
            return carry

        lax.fori_loop(0, count, body, 0)

    copies = []
    for k in range(seqs - 1):
        copies.append(
            remote(conv_in.at[seq_ids[k]], conv_r0.at[k], s0.at[0, k], r0.at[0, k], seq_place[k])
        )
        copies.append(
            remote(feed_in.at[seq_ids[k]], feed_r0.at[k], s0.at[1, k], r0.at[1, k], seq_place[k])
        )
    for copy in copies:
        copy.start()
    finish(copies)
    total(4 * high, conv_piece, conv_a1, lambda at: conv_in[me_seq, at], conv_r0)
    total(2 * high, feed_piece, feed_a1, lambda at: feed_in[me_seq, at], feed_r0)

    copies = []
    for k in (2, 1, 0):
        a, b = quad_ids[k]
        copies.append(
            remote(
                conv_a1.at[rows(a * 2 + b, conv_block)],
                conv_r1.at[k],
                s1.at[k],
                r1.at[k],
                quad_place[k],
            )
        )
    copies.append(
        remote(
            feed_a1.at[rows(quad_ids[0][1], feed_block)],
            feed_r1.at[0],
            s1.at[3],
            r1.at[3],
            quad_place[0],
        )
    )
    for copy in copies:
        copy.start()
    finish(copies)
    conv_at, feed_at = quad * conv_block, low * feed_block

    def own_conv(at):
        return conv_a1[pl.ds(pl.multiple_of(conv_at + at.start, conv_piece), conv_piece)]

    def own_feed(at):
        return feed_a1[pl.ds(pl.multiple_of(feed_at + at.start, feed_piece), feed_piece)]

    total(high, conv_piece, conv_a2, own_conv, conv_r1)
    total(high, feed_piece, feed_a2, own_feed, feed_r1)

    copies = []
    for k in range(high - 1):
        copies.append(
            remote(
                conv_a2.at[rows(high_ids[k], conv_piece)],
                conv_r2.at[k],
                s2.at[0, k],
                r2.at[0, k],
                high_place[k],
            )
        )
        copies.append(
            remote(
                feed_a2.at[rows(high_ids[k], feed_piece)],
                feed_r2.at[k],
                s2.at[1, k],
                r2.at[1, k],
                high_place[k],
            )
        )
    for copy in copies:
        copy.start()
    finish(copies)
    conv_mine = rows(quad * high + up, conv_piece)
    feed_mine = rows(low * high + up, feed_piece)
    value = conv_a2[rows(up, conv_piece)].astype(jnp.float32)
    for k in range(high - 1):
        value = value + conv_r2[k].astype(jnp.float32)
    conv_all[conv_mine] = value.astype(jnp.bfloat16)
    value = feed_a2[rows(up, feed_piece)].astype(jnp.float32)
    for k in range(high - 1):
        value = value + feed_r2[k].astype(jnp.float32)
    feed_all[feed_mine] = value.astype(jnp.bfloat16)

    copies = []
    for k in range(high - 1):
        copies.append(
            remote(
                conv_all.at[conv_mine], conv_all.at[conv_mine],
                s3.at[0, k], r3.at[0, k], high_place[k],
            )
        )
        copies.append(
            remote(
                feed_all.at[feed_mine], feed_all.at[feed_mine],
                s3.at[1, k], r3.at[1, k], high_place[k],
            )
        )
    for copy in copies:
        copy.start()
    finish(copies)

    copies = []
    for k in (2, 1, 0):
        mine = conv_all.at[rows(quad, conv_block)]
        copies.append(remote(mine, mine, s4.at[k], r4.at[k], quad_place[k]))
    mine = feed_all.at[rows(low, feed_block)]
    copies.append(remote(mine, mine, s4.at[3], r4.at[3], quad_place[0]))
    for copy in copies:
        copy.start()
    finish(copies)

    def widen(count, size, dest, source):
        def body(i, carry):
            at = rows(i, size)
            dest[at] = source[at].astype(jnp.float32)
            return carry

        lax.fori_loop(0, count, body, 0)

    widen(4 * high, conv_piece, conv_out, conv_all)
    widen(2 * high, feed_piece, feed_out, feed_all)


def summed(conv_pack, feed_pack):
    seqs = lax.axis_size("seq")
    high = lax.axis_size("dp") // 2
    conv_rows, feed_rows, cols = conv_pack.shape[1], feed_pack.shape[1], conv_pack.shape[2]
    conv_block, feed_block = conv_rows // 4, feed_rows // 2
    conv_piece, feed_piece = conv_block // high, feed_block // high
    low = jnp.bfloat16

    def buffer(*shape):
        return pltpu.VMEM(shape + (cols,), low)

    dma = pltpu.SemaphoreType.DMA
    return pl.pallas_call(
        functools.partial(reduce_kernel, seqs, high),
        out_shape=(
            jax.ShapeDtypeStruct((conv_rows, cols), jnp.float32),
            jax.ShapeDtypeStruct((feed_rows, cols), jnp.float32),
        ),
        in_specs=[pl.BlockSpec(memory_space=pltpu.VMEM)] * 2,
        out_specs=[pl.BlockSpec(memory_space=pltpu.VMEM)] * 2,
        scratch_shapes=[
            buffer(seqs - 1, conv_rows),
            buffer(seqs - 1, feed_rows),
            buffer(conv_rows),
            buffer(feed_rows),
            buffer(3, conv_block),
            buffer(1, feed_block),
            buffer(conv_block),
            buffer(feed_block),
            buffer(high - 1, conv_piece),
            buffer(high - 1, feed_piece),
            buffer(conv_rows),
            buffer(feed_rows),
            dma((2, seqs - 1)),
            dma((2, seqs - 1)),
            dma((4,)),
            dma((4,)),
            dma((2, high - 1)),
            dma((2, high - 1)),
            dma((2, high - 1)),
            dma((2, high - 1)),
            dma((4,)),
            dma((4,)),
        ],
        compiler_params=pltpu.CompilerParams(
            collective_id=0, has_side_effects=True, vmem_limit_bytes=40 * 2**20
        ),
    )(conv_pack, feed_pack)


def padded_rows(value, parts):
    unit = parts * 16
    extra = -value.shape[1] % unit
    return jnp.pad(value, ((0, 0), (0, extra), (0, 0)))


def reduced(conv_term, embed_term, in_term, out_term):
    seqs, dps = lax.axis_size("seq"), lax.axis_size("dp")
    taps, chans = conv_term.shape[0], conv_term.shape[1]
    part = chans // seqs
    hidden = in_term.shape[1]
    low = jnp.bfloat16
    conv_pack = conv_term.astype(low).reshape(taps, seqs, part, chans)
    conv_pack = conv_pack.transpose(1, 0, 2, 3).reshape(seqs, taps * part, chans)
    kinds = taps * BASES
    embed_pack = embed_term.astype(low).reshape(kinds, seqs, part).transpose(1, 0, 2)
    embed_pack = jnp.pad(embed_pack, ((0, 0), (0, 0), (0, chans - part)))
    conv_pack = padded_rows(jnp.concatenate([conv_pack, embed_pack], axis=1), 2 * dps)
    feed_pack = jnp.concatenate(
        [in_term.astype(low).reshape(seqs, part, hidden), out_term.astype(low).reshape(seqs, part, hidden)],
        axis=1,
    )
    feed_pack = padded_rows(feed_pack, dps)
    conv_sum, feed_sum = summed(conv_pack, feed_pack)
    grad_conv = conv_sum[: taps * part].reshape(taps, part, chans)
    grad_embed = conv_sum[taps * part : taps * part + kinds, :part].reshape(taps, BASES, part)
    return grad_embed, grad_conv, feed_sum[:part], feed_sum[part : 2 * part].T


def local(bases, embed, conv_w, w_in, w_out, cotangent):
    rows = bases.shape[1]
    chans = embed.shape[2]
    half = rows // 2
    padded_ids = padded(bases[0] + 1, (("seq", 0),), 2)
    levels = jnp.arange(1, BASES + 1, dtype=jnp.int32)
    onehots = [
        (padded_ids[k : k + rows, None] == levels[None, :]).astype(jnp.bfloat16)
        for k in range(TAPS)
    ]
    accum = jnp.zeros((rows, chans), jnp.float32)
    for k in range(TAPS):
        accum = accum + jnp.dot(onehots[k], embed[k], preferred_element_type=jnp.float32)
    h_zero = accum.astype(jnp.bfloat16)
    conv_full = lax.all_gather(conv_w, "seq", axis=1, tiled=True)
    h_padded = padded(h_zero, (("seq", 0),), 2)
    pre_conv = jnp.zeros((rows, chans), jnp.float32)
    for k in range(TAPS):
        pre_conv = pre_conv + jnp.dot(
            h_padded[k : k + rows], conv_full[k], preferred_element_type=jnp.float32
        )
    h_one = lax.optimization_barrier(
        (h_zero.astype(jnp.float32) + gelu_tanh(pre_conv)).astype(jnp.bfloat16)
    )
    h_onef = h_one.astype(jnp.float32)
    pooled = lax.optimization_barrier(
        (h_onef.reshape(half, 2, chans).sum(1) * 0.5).astype(jnp.bfloat16)
    )
    pooledf = pooled.astype(jnp.float32)
    scale = lax.rsqrt(jnp.mean(pooledf * pooledf, axis=-1, keepdims=True) + 1e-06)
    normed = (pooledf * scale).astype(jnp.bfloat16)
    in_rows, out_cols = (
        lax.all_gather(w_in, "seq", axis=0, tiled=True),
        lax.all_gather(w_out, "seq", axis=1, tiled=True),
    )
    dout = cotangent[0].astype(jnp.float32)
    dmixed = dout.reshape(half, 2, chans).sum(1).astype(jnp.bfloat16)
    both = jnp.concatenate([normed, partner_rows(normed)], axis=0)
    pre = jnp.dot(both, in_rows, preferred_element_type=jnp.float32)
    act = gelu_tanh(pre).astype(jnp.bfloat16)
    partial_value = jnp.dot(act, out_cols, preferred_element_type=jnp.float32)
    mixed = lax.optimization_barrier(
        (partial_value[:half] + partner_sums(partial_value[half:])).astype(jnp.bfloat16)
    )
    dmixed_both = jnp.concatenate([dmixed, partner_rows(dmixed)], axis=0)
    out_term = contract_rows(dmixed_both, act)
    dact = contract_cols(dmixed_both, out_cols)
    dpre = gelu_back(pre, dact).astype(jnp.bfloat16)
    in_term = contract_rows(both, dpre)
    dnormed_part = contract_cols(dpre, in_rows)
    dnormed = dnormed_part[:half] + partner_sums(dnormed_part[half:])
    output = (h_onef + jnp.repeat(mixed.astype(jnp.float32), 2, axis=0)).astype(jnp.bfloat16)
    dpooled = scale * dnormed - pooledf * scale**3 * jnp.mean(
        dnormed * pooledf, axis=-1, keepdims=True
    )
    dh_one = dout + jnp.repeat(dpooled * 0.5, 2, axis=0)
    dz_rows = gelu_back(pre_conv, dh_one).astype(jnp.bfloat16)
    dz_padded = padded(dz_rows, (("seq", 0),), 2)
    dh_zero = dh_one
    for k in range(TAPS):
        dh_zero = dh_zero + contract_cols(dz_padded[4 - k : 4 - k + rows], conv_full[k])
    conv_term = jnp.stack([contract_rows(h_padded[k : k + rows], dz_rows) for k in range(TAPS)])
    embed_term = jnp.stack(
        [
            lax.dot_general(
                onehots[k].astype(jnp.float32),
                dh_zero,
                (((0,), (0,)), ((), ())),
                precision=lax.Precision.HIGHEST,
                preferred_element_type=jnp.float32,
            )
            for k in range(TAPS)
        ]
    )
    grad_embed, grad_conv, grad_in, grad_out = reduced(conv_term, embed_term, in_term, out_term)
    return (output[None], grad_embed, grad_conv, grad_in, grad_out)


def solution(mesh):
    placed = (
        P(("dp", "sect"), "seq"),
        P(),
        P(None, "seq", None),
        P("seq", "sect"),
        P("sect", "seq"),
        P(("dp", "sect"), "seq", None),
    )
    return jax.shard_map(
        local,
        mesh=mesh,
        in_specs=placed,
        out_specs=(
            P(("dp", "sect"), "seq", None),
            P(None, None, "seq"),
            P(None, "seq", None),
            P("seq", "sect"),
            P("sect", "seq"),
        ),
        check_vma=False,
    )
```

```python
import functools

import jax
import jax.numpy as jnp
from jax import lax
from jax.experimental import pallas as pl
from jax.experimental.pallas import tpu as pltpu
from jax.sharding import PartitionSpec as P

TAPS = 5
BASES = 4


def swapped(value, axis, apart):
    mask = 2**apart
    pairs = [(source, source ^ mask) for source in range(lax.axis_size(axis))]
    return lax.ppermute(value, axis, pairs)


def padded(cells, sides, width):
    for axis, dim in sides:
        count = lax.axis_size(axis)
        ends = count - 1
        head = lax.slice_in_dim(cells, 0, width, axis=dim)
        tail = lax.slice_in_dim(cells, cells.shape[dim] - width, cells.shape[dim], axis=dim)
        cells = jnp.concatenate(
            [
                lax.ppermute(tail, axis, [(i, (i + 1) % count) for i in range(ends)]),
                cells,
                lax.ppermute(head, axis, [((i + 1) % count, i) for i in range(ends)]),
            ],
            axis=dim,
        )
    return cells


def gelu_tanh(value):
    return jax.nn.gelu(value, approximate=True)


def gelu_back(value, grad):
    unused, pull = jax.vjp(gelu_tanh, value)
    return pull(grad)[0]


def contract_rows(left, right):
    return lax.dot_general(
        left, right, (((0,), (0,)), ((), ())), preferred_element_type=jnp.float32
    )


def contract_cols(left, right):
    return lax.dot_general(
        left, right, (((1,), (1,)), ((), ())), preferred_element_type=jnp.float32
    )


def partner_rows(value):
    return swapped(value, "sect", 0)


def partner_sums(value):
    return swapped(value.astype(jnp.bfloat16), "sect", 0).astype(value.dtype)


def remote(src, dst, send, recv, place):
    return pltpu.make_async_remote_copy(
        src_ref=src,
        dst_ref=dst,
        send_sem=send,
        recv_sem=recv,
        device_id=place,
        device_id_type=pl.DeviceIdType.MESH,
    )


def reduce_kernel(
    seqs, high, conv_in, feed_in, conv_out, feed_out,
    conv_r0, feed_r0, conv_a1, feed_a1, conv_r1, feed_r1, conv_a2, feed_a2,
    conv_r2, feed_r2, conv_all, feed_all,
    s0, r0, s1, r1, s2, r2, s3, r3, s4, r4,
):
    me_seq = lax.axis_index("seq")
    me_sect = lax.axis_index("sect")
    me_dp = lax.axis_index("dp")
    low = lax.rem(me_dp, 2)
    up = me_dp // 2
    quad = me_sect * 2 + low
    conv_block, feed_block = conv_a2.shape[0], feed_a2.shape[0]
    conv_piece, feed_piece = conv_r2.shape[1], feed_r2.shape[1]

    seq_ids = [lax.rem(me_seq + k, seqs) for k in range(1, seqs)]
    quad_ids = [(k // 2, k % 2) for k in range(1, 4)]
    quad_ids = [
        (lax.rem(me_sect + a, 2), lax.rem(low + b, 2)) for a, b in quad_ids
    ]
    high_ids = [lax.rem(up + k, high) for k in range(1, high)]
    seq_place = [{"seq": p} for p in seq_ids]
    quad_place = [{"sect": a, "dp": up * 2 + b} for a, b in quad_ids]
    high_place = [{"dp": p * 2 + low} for p in high_ids]

    barrier = pltpu.get_barrier_semaphore()
    for place in seq_place + quad_place + high_place:
        pl.semaphore_signal(
            barrier, inc=1, device_id=place, device_id_type=pl.DeviceIdType.MESH
        )
    pl.semaphore_wait(barrier, len(seq_place) + len(quad_place) + len(high_place))

    def rows(index, size):
        return pl.ds(pl.multiple_of(index * size, size), size)

    def finish(copies):
        for copy in copies:
            copy.wait_recv()
        for copy in copies:
            copy.wait_send()

    def total(count, size, dest, own, slots):
        def body(i, carry):
            at = rows(i, size)
            value = own(at).astype(jnp.float32)
            for slot in range(slots.shape[0]):
                value = value + slots[slot, at].astype(jnp.float32)
            dest[at] = value.astype(dest.dtype)
            return carry

        lax.fori_loop(0, count, body, 0)

    copies = []
    for k in range(seqs - 1):
        copies.append(
            remote(conv_in.at[seq_ids[k]], conv_r0.at[k], s0.at[0, k], r0.at[0, k], seq_place[k])
        )
        copies.append(
            remote(feed_in.at[seq_ids[k]], feed_r0.at[k], s0.at[1, k], r0.at[1, k], seq_place[k])
        )
    for copy in copies:
        copy.start()
    finish(copies)
    total(4 * high, conv_piece, conv_a1, lambda at: conv_in[me_seq, at], conv_r0)
    total(2 * high, feed_piece, feed_a1, lambda at: feed_in[me_seq, at], feed_r0)

    copies = []
    for k in (2, 1, 0):
        a, b = quad_ids[k]
        copies.append(
            remote(
                conv_a1.at[rows(a * 2 + b, conv_block)],
                conv_r1.at[k],
                s1.at[k],
                r1.at[k],
                quad_place[k],
            )
        )
    copies.append(
        remote(
            feed_a1.at[rows(quad_ids[0][1], feed_block)],
            feed_r1.at[0],
            s1.at[3],
            r1.at[3],
            quad_place[0],
        )
    )
    for copy in copies:
        copy.start()
    finish(copies)
    conv_at, feed_at = quad * conv_block, low * feed_block

    def own_conv(at):
        return conv_a1[pl.ds(pl.multiple_of(conv_at + at.start, conv_piece), conv_piece)]

    def own_feed(at):
        return feed_a1[pl.ds(pl.multiple_of(feed_at + at.start, feed_piece), feed_piece)]

    total(high, conv_piece, conv_a2, own_conv, conv_r1)
    total(high, feed_piece, feed_a2, own_feed, feed_r1)

    copies = []
    for k in range(high - 1):
        copies.append(
            remote(
                conv_a2.at[rows(high_ids[k], conv_piece)],
                conv_r2.at[k],
                s2.at[0, k],
                r2.at[0, k],
                high_place[k],
            )
        )
        copies.append(
            remote(
                feed_a2.at[rows(high_ids[k], feed_piece)],
                feed_r2.at[k],
                s2.at[1, k],
                r2.at[1, k],
                high_place[k],
            )
        )
    for copy in copies:
        copy.start()
    finish(copies)
    conv_mine = rows(quad * high + up, conv_piece)
    feed_mine = rows(low * high + up, feed_piece)
    value = conv_a2[rows(up, conv_piece)].astype(jnp.float32)
    for k in range(high - 1):
        value = value + conv_r2[k].astype(jnp.float32)
    conv_all[conv_mine] = value.astype(jnp.bfloat16)
    value = feed_a2[rows(up, feed_piece)].astype(jnp.float32)
    for k in range(high - 1):
        value = value + feed_r2[k].astype(jnp.float32)
    feed_all[feed_mine] = value.astype(jnp.bfloat16)

    copies = []
    for k in range(high - 1):
        copies.append(
            remote(
                conv_all.at[conv_mine], conv_all.at[conv_mine],
                s3.at[0, k], r3.at[0, k], high_place[k],
            )
        )
        copies.append(
            remote(
                feed_all.at[feed_mine], feed_all.at[feed_mine],
                s3.at[1, k], r3.at[1, k], high_place[k],
            )
        )
    for copy in copies:
        copy.start()
    finish(copies)

    copies = []
    for k in (2, 1, 0):
        mine = conv_all.at[rows(quad, conv_block)]
        copies.append(remote(mine, mine, s4.at[k], r4.at[k], quad_place[k]))
    mine = feed_all.at[rows(low, feed_block)]
    copies.append(remote(mine, mine, s4.at[3], r4.at[3], quad_place[0]))
    for copy in copies:
        copy.start()
    finish(copies)

    def widen(count, size, dest, source):
        def body(i, carry):
            at = rows(i, size)
            dest[at] = source[at].astype(jnp.float32)
            return carry

        lax.fori_loop(0, count, body, 0)

    widen(4 * high, conv_piece, conv_out, conv_all)
    widen(2 * high, feed_piece, feed_out, feed_all)


def summed(conv_pack, feed_pack):
    seqs = lax.axis_size("seq")
    high = lax.axis_size("dp") // 2
    conv_rows, feed_rows, cols = conv_pack.shape[1], feed_pack.shape[1], conv_pack.shape[2]
    conv_block, feed_block = conv_rows // 4, feed_rows // 2
    conv_piece, feed_piece = conv_block // high, feed_block // high
    low = jnp.bfloat16

    def buffer(*shape):
        return pltpu.VMEM(shape + (cols,), low)

    dma = pltpu.SemaphoreType.DMA
    return pl.pallas_call(
        functools.partial(reduce_kernel, seqs, high),
        out_shape=(
            jax.ShapeDtypeStruct((conv_rows, cols), jnp.float32),
            jax.ShapeDtypeStruct((feed_rows, cols), jnp.float32),
        ),
        in_specs=[pl.BlockSpec(memory_space=pltpu.VMEM)] * 2,
        out_specs=[pl.BlockSpec(memory_space=pltpu.VMEM)] * 2,
        scratch_shapes=[
            buffer(seqs - 1, conv_rows),
            buffer(seqs - 1, feed_rows),
            buffer(conv_rows),
            buffer(feed_rows),
            buffer(3, conv_block),
            buffer(1, feed_block),
            buffer(conv_block),
            buffer(feed_block),
            buffer(high - 1, conv_piece),
            buffer(high - 1, feed_piece),
            buffer(conv_rows),
            buffer(feed_rows),
            dma((2, seqs - 1)),
            dma((2, seqs - 1)),
            dma((4,)),
            dma((4,)),
            dma((2, high - 1)),
            dma((2, high - 1)),
            dma((2, high - 1)),
            dma((2, high - 1)),
            dma((4,)),
            dma((4,)),
        ],
        compiler_params=pltpu.CompilerParams(
            collective_id=0, has_side_effects=True, vmem_limit_bytes=40 * 2**20
        ),
    )(conv_pack, feed_pack)


def padded_rows(value, parts):
    unit = parts * 16
    extra = -value.shape[1] % unit
    return jnp.pad(value, ((0, 0), (0, extra), (0, 0)))


def reduced(conv_term, embed_term, in_term, out_term):
    seqs, dps = lax.axis_size("seq"), lax.axis_size("dp")
    taps, chans = conv_term.shape[0], conv_term.shape[1]
    part = chans // seqs
    hidden = in_term.shape[1]
    low = jnp.bfloat16
    conv_pack = conv_term.astype(low).reshape(taps, seqs, part, chans)
    conv_pack = conv_pack.transpose(1, 0, 2, 3).reshape(seqs, taps * part, chans)
    kinds = taps * BASES
    embed_pack = embed_term.astype(low).reshape(kinds, seqs, part).transpose(1, 0, 2)
    embed_pack = jnp.pad(embed_pack, ((0, 0), (0, 0), (0, chans - part)))
    conv_pack = padded_rows(jnp.concatenate([conv_pack, embed_pack], axis=1), 2 * dps)
    feed_pack = jnp.concatenate(
        [in_term.astype(low).reshape(seqs, part, hidden), out_term.astype(low).reshape(seqs, part, hidden)],
        axis=1,
    )
    feed_pack = padded_rows(feed_pack, dps)
    conv_sum, feed_sum = summed(conv_pack, feed_pack)
    grad_conv = conv_sum[: taps * part].reshape(taps, part, chans)
    grad_embed = conv_sum[taps * part : taps * part + kinds, :part].reshape(taps, BASES, part)
    return grad_embed, grad_conv, feed_sum[:part], feed_sum[part : 2 * part].T


def gather_kernel(
    seqs, conv_w, in_w, out_w, ids, dmixed, conv_full, in_full, out_full, ids_near, both,
    send, recv, id_send, id_recv, row_send, row_recv,
):
    me = lax.axis_index("seq")
    peers = [{"seq": lax.rem(me + k, seqs)} for k in range(1, seqs)]
    partner = {"sect": 1 - lax.axis_index("sect")}
    barrier = pltpu.get_barrier_semaphore()
    for place in peers + [partner]:
        pl.semaphore_signal(
            barrier, inc=1, device_id=place, device_id_type=pl.DeviceIdType.MESH
        )
    pl.semaphore_wait(barrier, len(peers) + 1)
    part, half = in_w.shape[0], dmixed.shape[0]
    mine = pl.ds(pl.multiple_of(me * part, part), part)
    copies = [
        remote(ids, ids_near.at[0], id_send.at[0], id_recv.at[0], peers[0]),
        remote(ids, ids_near.at[1], id_send.at[1], id_recv.at[1], peers[-1]),
        remote(dmixed, both.at[pl.ds(half, half)], row_send, row_recv, partner),
    ]
    for k, place in enumerate(peers):
        copies += [
            remote(conv_w, conv_full.at[:, mine], send.at[0, k], recv.at[0, k], place),
            remote(in_w, in_full.at[mine], send.at[1, k], recv.at[1, k], place),
            remote(out_w, out_full.at[mine], send.at[2, k], recv.at[2, k], place),
        ]
    for copy in copies:
        copy.start()
    for tap in range(conv_w.shape[0]):
        conv_full[tap, mine] = conv_w[tap]
    in_full[mine] = in_w[...]
    out_full[mine] = out_w[...]
    both[pl.ds(0, half)] = dmixed[...]
    for copy in copies:
        copy.wait_recv()
    for copy in copies:
        copy.wait_send()


def gathered(conv_w, in_w, out_w, ids, dmixed):
    seqs = lax.axis_size("seq")
    taps, part, chans = conv_w.shape
    low = jnp.bfloat16
    dma = pltpu.SemaphoreType.DMA
    return pl.pallas_call(
        functools.partial(gather_kernel, seqs),
        out_shape=(
            jax.ShapeDtypeStruct((taps, part * seqs, chans), low),
            jax.ShapeDtypeStruct((part * seqs, in_w.shape[1]), low),
            jax.ShapeDtypeStruct((part * seqs, out_w.shape[1]), low),
            jax.ShapeDtypeStruct((2,) + ids.shape, jnp.int32),
            jax.ShapeDtypeStruct((2 * dmixed.shape[0], chans), low),
        ),
        in_specs=[pl.BlockSpec(memory_space=pltpu.VMEM)] * 5,
        out_specs=[pl.BlockSpec(memory_space=pltpu.VMEM)] * 5,
        scratch_shapes=[
            dma((3, seqs - 1)),
            dma((3, seqs - 1)),
            dma((2,)),
            dma((2,)),
            dma(()),
            dma(()),
        ],
        compiler_params=pltpu.CompilerParams(
            collective_id=1, has_side_effects=True, vmem_limit_bytes=32 * 2**20
        ),
    )(conv_w, in_w, out_w, ids, dmixed)


def local(bases, embed, conv_w, w_in, w_out, cotangent):
    rows = bases.shape[1]
    chans = embed.shape[2]
    half = rows // 2
    seq, ends = lax.axis_index("seq"), lax.axis_size("seq") - 1
    ids = bases + 1
    dout = cotangent[0].astype(jnp.float32)
    dmixed = dout.reshape(half, 2, chans).sum(1).astype(jnp.bfloat16)
    conv_full, in_rows, out_rows, ids_near, dmixed_both = gathered(
        conv_w, w_in, w_out.T, ids, dmixed
    )
    before = jnp.where(seq > 0, ids_near[0, 0, rows - 4 :], 0)
    after = jnp.where(seq < ends, ids_near[1, 0, :4], 0)
    padded_ids = jnp.concatenate([before, ids[0], after])
    levels = jnp.arange(1, BASES + 1, dtype=jnp.int32)
    wide_hots = jnp.concatenate(
        [
            (padded_ids[k : k + rows + 4, None] == levels[None, :]).astype(jnp.bfloat16)
            for k in range(TAPS)
        ],
        axis=1,
    )
    accum = jnp.dot(
        wide_hots, embed.reshape(TAPS * BASES, chans), preferred_element_type=jnp.float32
    )
    place = jnp.arange(rows + 4)[:, None]
    inside = ((place >= 2) | (seq > 0)) & ((place < rows + 2) | (seq < ends))
    h_padded = jnp.where(inside, accum, 0.0).astype(jnp.bfloat16)
    h_zero = h_padded[2 : 2 + rows]
    pre_conv = jnp.zeros((rows, chans), jnp.float32)
    for k in range(TAPS):
        pre_conv = pre_conv + jnp.dot(
            h_padded[k : k + rows], conv_full[k], preferred_element_type=jnp.float32
        )
    h_one = lax.optimization_barrier(
        (h_zero.astype(jnp.float32) + gelu_tanh(pre_conv)).astype(jnp.bfloat16)
    )
    h_onef = h_one.astype(jnp.float32)
    pooled = lax.optimization_barrier(
        (h_onef.reshape(half, 2, chans).sum(1) * 0.5).astype(jnp.bfloat16)
    )
    pooledf = pooled.astype(jnp.float32)
    scale = lax.rsqrt(jnp.mean(pooledf * pooledf, axis=-1, keepdims=True) + 1e-06)
    normed = (pooledf * scale).astype(jnp.bfloat16)
    both = jnp.concatenate([normed, partner_rows(normed)], axis=0)
    pre = jnp.dot(both, in_rows, preferred_element_type=jnp.float32)
    act = gelu_tanh(pre).astype(jnp.bfloat16)
    partial_value = contract_cols(act, out_rows)
    mixed = lax.optimization_barrier(
        (partial_value[:half] + partner_sums(partial_value[half:])).astype(jnp.bfloat16)
    )
    out_term = contract_rows(dmixed_both, act)
    dact = jnp.dot(dmixed_both, out_rows, preferred_element_type=jnp.float32)
    dpre = gelu_back(pre, dact).astype(jnp.bfloat16)
    in_term = contract_rows(both, dpre)
    dnormed_part = contract_cols(dpre, in_rows)
    dnormed = dnormed_part[:half] + partner_sums(dnormed_part[half:])
    output = (h_onef + jnp.repeat(mixed.astype(jnp.float32), 2, axis=0)).astype(jnp.bfloat16)
    dpooled = scale * dnormed - pooledf * scale**3 * jnp.mean(
        dnormed * pooledf, axis=-1, keepdims=True
    )
    dh_one = dout + jnp.repeat(dpooled * 0.5, 2, axis=0)
    dz_rows = gelu_back(pre_conv, dh_one).astype(jnp.bfloat16)
    dz_padded = padded(dz_rows, (("seq", 0),), 2)
    dh_zero = dh_one
    for k in range(TAPS):
        dh_zero = dh_zero + contract_cols(dz_padded[4 - k : 4 - k + rows], conv_full[k])
    conv_term = jnp.stack([contract_rows(h_padded[k : k + rows], dz_rows) for k in range(TAPS)])
    embed_term = lax.dot_general(
        wide_hots[2 : 2 + rows].astype(jnp.float32),
        dh_zero,
        (((0,), (0,)), ((), ())),
        precision=lax.Precision.HIGHEST,
        preferred_element_type=jnp.float32,
    )
    grad_embed, grad_conv, grad_in, grad_out = reduced(conv_term, embed_term, in_term, out_term)
    return (output[None], grad_embed, grad_conv, grad_in, grad_out)


def solution(mesh):
    placed = (
        P(("dp", "sect"), "seq"),
        P(),
        P(None, "seq", None),
        P("seq", "sect"),
        P("sect", "seq"),
        P(("dp", "sect"), "seq", None),
    )
    return jax.shard_map(
        local,
        mesh=mesh,
        in_specs=placed,
        out_specs=(
            P(("dp", "sect"), "seq", None),
            P(None, None, "seq"),
            P(None, "seq", None),
            P("seq", "sect"),
            P("sect", "seq"),
        ),
        check_vma=False,
    )
```

```python
import functools

import jax
import jax.numpy as jnp
from jax import lax
from jax.experimental import pallas as pl
from jax.experimental.pallas import tpu as pltpu
from jax.sharding import PartitionSpec as P

TAPS = 5
BASES = 4


def swapped(value, axis, apart):
    mask = 2**apart
    pairs = [(source, source ^ mask) for source in range(lax.axis_size(axis))]
    return lax.ppermute(value, axis, pairs)


def padded(cells, sides, width):
    for axis, dim in sides:
        count = lax.axis_size(axis)
        ends = count - 1
        head = lax.slice_in_dim(cells, 0, width, axis=dim)
        tail = lax.slice_in_dim(cells, cells.shape[dim] - width, cells.shape[dim], axis=dim)
        cells = jnp.concatenate(
            [
                lax.ppermute(tail, axis, [(i, (i + 1) % count) for i in range(ends)]),
                cells,
                lax.ppermute(head, axis, [((i + 1) % count, i) for i in range(ends)]),
            ],
            axis=dim,
        )
    return cells


def gelu_tanh(value):
    return jax.nn.gelu(value, approximate=True)


def gelu_back(value, grad):
    unused, pull = jax.vjp(gelu_tanh, value)
    return pull(grad)[0]


def contract_rows(left, right):
    return lax.dot_general(
        left, right, (((0,), (0,)), ((), ())), preferred_element_type=jnp.float32
    )


def contract_cols(left, right):
    return lax.dot_general(
        left, right, (((1,), (1,)), ((), ())), preferred_element_type=jnp.float32
    )


def partner_rows(value):
    return swapped(value, "sect", 0)


def partner_sums(value):
    return swapped(value.astype(jnp.bfloat16), "sect", 0).astype(value.dtype)


def remote(src, dst, send, recv, place):
    return pltpu.make_async_remote_copy(
        src_ref=src,
        dst_ref=dst,
        send_sem=send,
        recv_sem=recv,
        device_id=place,
        device_id_type=pl.DeviceIdType.MESH,
    )


def reduce_kernel(seqs, high, conv_in, feed_in, conv_out, feed_out, send, recv, *buffers):
    me_seq = lax.axis_index("seq")
    me_sect = lax.axis_index("sect")
    me_dp = lax.axis_index("dp")
    low = lax.rem(me_dp, 2)
    up = me_dp // 2
    quad = me_sect * 2 + low
    seq_ids = [lax.rem(me_seq + k, seqs) for k in range(1, seqs)]
    quad_ids = [(k // 2, k % 2) for k in range(1, 4)]
    quad_ids = [
        (lax.rem(me_sect + a, 2), lax.rem(low + b, 2)) for a, b in quad_ids
    ]
    high_ids = [lax.rem(up + k, high) for k in range(1, high)]
    seq_place = [{"seq": p} for p in seq_ids]
    quad_place = [{"sect": a, "dp": up * 2 + b} for a, b in quad_ids]
    high_place = [{"dp": p * 2 + low} for p in high_ids]

    barrier = pltpu.get_barrier_semaphore()
    for place in seq_place + quad_place + high_place:
        pl.semaphore_signal(
            barrier, inc=1, device_id=place, device_id_type=pl.DeviceIdType.MESH
        )
    pl.semaphore_wait(barrier, len(seq_place) + len(quad_place) + len(high_place))

    def rows(index, size):
        return pl.ds(pl.multiple_of(index * size, size), size)

    def finish(copies):
        for copy in copies:
            copy.wait_recv()
        for copy in copies:
            copy.wait_send()

    def total(count, size, dest, own, slots):
        def body(i, carry):
            at = rows(i, size)
            value = own(at).astype(jnp.float32)
            for slot in range(slots.shape[0]):
                value = value + slots[slot, at].astype(jnp.float32)
            dest[at] = value.astype(dest.dtype)
            return carry

        lax.fori_loop(0, count, body, 0)

    quads = (quad, [(a * 2 + b, p) for (a, b), p in zip(quad_ids, quad_place)])
    highs = (up, list(zip(high_ids, high_place)))
    lows = (low, [(quad_ids[0][1], quad_place[0])])
    half = conv_in.shape[1] // 2
    plans = [
        (conv_in, conv_out, 0, quads, highs),
        (conv_in, conv_out, half, highs, quads),
        (feed_in, feed_out, 0, lows, highs),
    ]
    streams = [plan + tuple(buffers[6 * n : 6 * n + 6]) for n, plan in enumerate(plans)]

    def exchange(phase, pairs):
        copies = []
        for n, stream in enumerate(streams):
            for k, (src, dst, place) in enumerate(pairs(stream)):
                at = n * 5 + phase, k
                copies.append(remote(src, dst, send.at[at], recv.at[at], place))
        for copy in copies:
            copy.start()
        finish(copies)

    def scatter_seq(stream):
        source, out, base, first, second, r0, a1, r1, a2, r2, full = stream
        return [
            (source.at[peer, pl.ds(base, a1.shape[0])], r0.at[k], place)
            for k, (peer, place) in enumerate(zip(seq_ids, seq_place))
        ]

    def scatter_first(stream):
        source, out, base, first, second, r0, a1, r1, a2, r2, full = stream
        return [
            (a1.at[rows(peer, a2.shape[0])], r1.at[k], place)
            for k, (peer, place) in enumerate(first[1])
        ]

    def scatter_second(stream):
        source, out, base, first, second, r0, a1, r1, a2, r2, full = stream
        return [
            (a2.at[rows(peer, r2.shape[1])], r2.at[k], place)
            for k, (peer, place) in enumerate(second[1])
        ]

    def mine_of(stream):
        source, out, base, first, second, r0, a1, r1, a2, r2, full = stream
        piece = r2.shape[1]
        return rows(first[0] * (a2.shape[0] // piece) + second[0], piece)

    def gather_second(stream):
        part = stream[-1].at[mine_of(stream)]
        return [(part, part, place) for peer, place in stream[4][1]]

    def gather_first(stream):
        part = stream[-1].at[rows(stream[3][0], stream[8].shape[0])]
        return [(part, part, place) for peer, place in stream[3][1]]

    def add(piece, count, dest, own, slots):
        def body(i, carry):
            at = rows(i, piece)
            value = own(i * piece, piece).astype(jnp.float32)
            for slot in range(slots.shape[0]):
                value = value + slots[slot, at].astype(jnp.float32)
            dest[at] = value.astype(dest.dtype)
            return carry

        lax.fori_loop(0, count, body, 0)

    def at_rows(start, size):
        return pl.ds(pl.multiple_of(start, 16), size)

    exchange(0, scatter_seq)
    for source, out, base, first, second, r0, a1, r1, a2, r2, full in streams:
        piece = r2.shape[1]
        add(
            piece, a1.shape[0] // piece, a1,
            lambda at, size, source=source, base=base: source[me_seq, at_rows(base + at, size)],
            r0,
        )
    exchange(1, scatter_first)
    for source, out, base, first, second, r0, a1, r1, a2, r2, full in streams:
        piece, start = r2.shape[1], first[0] * a2.shape[0]
        add(
            piece, a2.shape[0] // piece, a2,
            lambda at, size, a1=a1, start=start: a1[at_rows(start + at, size)],
            r1,
        )
    exchange(2, scatter_second)
    for stream in streams:
        a2, r2, full = stream[-3:]
        value = a2[rows(stream[4][0], r2.shape[1])].astype(jnp.float32)
        for k in range(r2.shape[0]):
            value = value + r2[k].astype(jnp.float32)
        full[mine_of(stream)] = value.astype(jnp.bfloat16)
    exchange(3, gather_second)
    exchange(4, gather_first)
    for source, out, base, first, second, r0, a1, r1, a2, r2, full in streams:
        piece = r2.shape[1]

        def widen(i, carry, out=out, base=base, full=full, piece=piece):
            out[at_rows(base + i * piece, piece)] = full[rows(i, piece)].astype(jnp.float32)
            return carry

        lax.fori_loop(0, full.shape[0] // piece, widen, 0)


def summed(conv_pack, feed_pack):
    seqs = lax.axis_size("seq")
    high = lax.axis_size("dp") // 2
    conv_rows, feed_rows, cols = conv_pack.shape[1], feed_pack.shape[1], conv_pack.shape[2]
    low = jnp.bfloat16

    def buffer(*shape):
        return pltpu.VMEM(shape + (cols,), low)

    def stream(count, first, second):
        block = count // first
        return [
            buffer(seqs - 1, count),
            buffer(count),
            buffer(first - 1, block),
            buffer(block),
            buffer(second - 1, block // second),
            buffer(count),
        ]

    dma = pltpu.SemaphoreType.DMA
    peers = max(seqs - 1, 3, high - 1)
    return pl.pallas_call(
        functools.partial(reduce_kernel, seqs, high),
        out_shape=(
            jax.ShapeDtypeStruct((conv_rows, cols), jnp.float32),
            jax.ShapeDtypeStruct((feed_rows, cols), jnp.float32),
        ),
        in_specs=[pl.BlockSpec(memory_space=pltpu.VMEM)] * 2,
        out_specs=[pl.BlockSpec(memory_space=pltpu.VMEM)] * 2,
        scratch_shapes=[
            dma((15, peers)),
            dma((15, peers)),
            *stream(conv_rows // 2, 4, high),
            *stream(conv_rows // 2, high, 4),
            *stream(feed_rows, 2, high),
        ],
        compiler_params=pltpu.CompilerParams(
            collective_id=0, has_side_effects=True, vmem_limit_bytes=40 * 2**20
        ),
    )(conv_pack, feed_pack)


def padded_rows(value, parts):
    unit = parts * 16
    extra = -value.shape[1] % unit
    return jnp.pad(value, ((0, 0), (0, extra), (0, 0)))


def reduced(conv_term, embed_term, in_term, out_term):
    seqs, dps = lax.axis_size("seq"), lax.axis_size("dp")
    taps, chans = conv_term.shape[0], conv_term.shape[1]
    part = chans // seqs
    hidden = in_term.shape[1]
    low = jnp.bfloat16
    conv_pack = conv_term.astype(low).reshape(taps, seqs, part, chans)
    conv_pack = conv_pack.transpose(1, 0, 2, 3).reshape(seqs, taps * part, chans)
    kinds = taps * BASES
    embed_pack = embed_term.astype(low).reshape(kinds, seqs, part).transpose(1, 0, 2)
    embed_pack = jnp.pad(embed_pack, ((0, 0), (0, 0), (0, chans - part)))
    conv_pack = padded_rows(jnp.concatenate([conv_pack, embed_pack], axis=1), 4 * dps)
    feed_pack = jnp.concatenate(
        [in_term.astype(low).reshape(seqs, part, hidden), out_term.astype(low).reshape(seqs, part, hidden)],
        axis=1,
    )
    feed_pack = padded_rows(feed_pack, dps)
    conv_sum, feed_sum = summed(conv_pack, feed_pack)
    grad_conv = conv_sum[: taps * part].reshape(taps, part, chans)
    grad_embed = conv_sum[taps * part : taps * part + kinds, :part].reshape(taps, BASES, part)
    return grad_embed, grad_conv, feed_sum[:part], feed_sum[part : 2 * part].T


def gather_kernel(
    seqs, conv_w, in_w, out_w, ids, dmixed, conv_full, in_full, out_full, ids_near, both,
    send, recv, id_send, id_recv, row_send, row_recv,
):
    me = lax.axis_index("seq")
    peers = [{"seq": lax.rem(me + k, seqs)} for k in range(1, seqs)]
    partner = {"sect": 1 - lax.axis_index("sect")}
    barrier = pltpu.get_barrier_semaphore()
    for place in peers + [partner]:
        pl.semaphore_signal(
            barrier, inc=1, device_id=place, device_id_type=pl.DeviceIdType.MESH
        )
    pl.semaphore_wait(barrier, len(peers) + 1)
    part, half = in_w.shape[0], dmixed.shape[0]
    mine = pl.ds(pl.multiple_of(me * part, part), part)
    copies = [
        remote(ids, ids_near.at[0], id_send.at[0], id_recv.at[0], peers[0]),
        remote(ids, ids_near.at[1], id_send.at[1], id_recv.at[1], peers[-1]),
        remote(dmixed, both.at[pl.ds(half, half)], row_send, row_recv, partner),
    ]
    for k, place in enumerate(peers):
        copies += [
            remote(conv_w, conv_full.at[:, mine], send.at[0, k], recv.at[0, k], place),
            remote(in_w, in_full.at[mine], send.at[1, k], recv.at[1, k], place),
            remote(out_w, out_full.at[mine], send.at[2, k], recv.at[2, k], place),
        ]
    for copy in copies:
        copy.start()
    for tap in range(conv_w.shape[0]):
        conv_full[tap, mine] = conv_w[tap]
    in_full[mine] = in_w[...]
    out_full[mine] = out_w[...]
    both[pl.ds(0, half)] = dmixed[...]
    for copy in copies:
        copy.wait_recv()
    for copy in copies:
        copy.wait_send()


def gathered(conv_w, in_w, out_w, ids, dmixed):
    seqs = lax.axis_size("seq")
    taps, part, chans = conv_w.shape
    low = jnp.bfloat16
    dma = pltpu.SemaphoreType.DMA
    return pl.pallas_call(
        functools.partial(gather_kernel, seqs),
        out_shape=(
            jax.ShapeDtypeStruct((taps, part * seqs, chans), low),
            jax.ShapeDtypeStruct((part * seqs, in_w.shape[1]), low),
            jax.ShapeDtypeStruct((part * seqs, out_w.shape[1]), low),
            jax.ShapeDtypeStruct((2,) + ids.shape, jnp.int32),
            jax.ShapeDtypeStruct((2 * dmixed.shape[0], chans), low),
        ),
        in_specs=[pl.BlockSpec(memory_space=pltpu.VMEM)] * 5,
        out_specs=[pl.BlockSpec(memory_space=pltpu.VMEM)] * 5,
        scratch_shapes=[
            dma((3, seqs - 1)),
            dma((3, seqs - 1)),
            dma((2,)),
            dma((2,)),
            dma(()),
            dma(()),
        ],
        compiler_params=pltpu.CompilerParams(
            collective_id=1, has_side_effects=True, vmem_limit_bytes=32 * 2**20
        ),
    )(conv_w, in_w, out_w, ids, dmixed)


def local(bases, embed, conv_w, w_in, w_out, cotangent):
    rows = bases.shape[1]
    chans = embed.shape[2]
    half = rows // 2
    seq, ends = lax.axis_index("seq"), lax.axis_size("seq") - 1
    ids = bases + 1
    dout = cotangent[0].astype(jnp.float32)
    dmixed = dout.reshape(half, 2, chans).sum(1).astype(jnp.bfloat16)
    conv_full, in_rows, out_rows, ids_near, dmixed_both = gathered(
        conv_w, w_in, w_out.T, ids, dmixed
    )
    before = jnp.where(seq > 0, ids_near[0, 0, rows - 4 :], 0)
    after = jnp.where(seq < ends, ids_near[1, 0, :4], 0)
    padded_ids = jnp.concatenate([before, ids[0], after])
    levels = jnp.arange(1, BASES + 1, dtype=jnp.int32)
    wide_hots = jnp.concatenate(
        [
            (padded_ids[k : k + rows + 4, None] == levels[None, :]).astype(jnp.bfloat16)
            for k in range(TAPS)
        ],
        axis=1,
    )
    accum = jnp.dot(
        wide_hots, embed.reshape(TAPS * BASES, chans), preferred_element_type=jnp.float32
    )
    place = jnp.arange(rows + 4)[:, None]
    inside = ((place >= 2) | (seq > 0)) & ((place < rows + 2) | (seq < ends))
    h_padded = jnp.where(inside, accum, 0.0).astype(jnp.bfloat16)
    h_zero = h_padded[2 : 2 + rows]
    pre_conv = jnp.zeros((rows, chans), jnp.float32)
    for k in range(TAPS):
        pre_conv = pre_conv + jnp.dot(
            h_padded[k : k + rows], conv_full[k], preferred_element_type=jnp.float32
        )
    h_one = lax.optimization_barrier(
        (h_zero.astype(jnp.float32) + gelu_tanh(pre_conv)).astype(jnp.bfloat16)
    )
    h_onef = h_one.astype(jnp.float32)
    pooled = lax.optimization_barrier(
        (h_onef.reshape(half, 2, chans).sum(1) * 0.5).astype(jnp.bfloat16)
    )
    pooledf = pooled.astype(jnp.float32)
    scale = lax.rsqrt(jnp.mean(pooledf * pooledf, axis=-1, keepdims=True) + 1e-06)
    normed = (pooledf * scale).astype(jnp.bfloat16)
    both = jnp.concatenate([normed, partner_rows(normed)], axis=0)
    pre = jnp.dot(both, in_rows, preferred_element_type=jnp.float32)
    act = gelu_tanh(pre).astype(jnp.bfloat16)
    partial_value = contract_cols(act, out_rows)
    mixed = lax.optimization_barrier(
        (partial_value[:half] + partner_sums(partial_value[half:])).astype(jnp.bfloat16)
    )
    out_term = contract_rows(dmixed_both, act)
    dact = jnp.dot(dmixed_both, out_rows, preferred_element_type=jnp.float32)
    dpre = gelu_back(pre, dact).astype(jnp.bfloat16)
    in_term = contract_rows(both, dpre)
    dnormed_part = contract_cols(dpre, in_rows)
    dnormed = dnormed_part[:half] + partner_sums(dnormed_part[half:])
    output = (h_onef + jnp.repeat(mixed.astype(jnp.float32), 2, axis=0)).astype(jnp.bfloat16)
    dpooled = scale * dnormed - pooledf * scale**3 * jnp.mean(
        dnormed * pooledf, axis=-1, keepdims=True
    )
    dh_one = dout + jnp.repeat(dpooled * 0.5, 2, axis=0)
    dz_rows = gelu_back(pre_conv, dh_one).astype(jnp.bfloat16)
    dz_padded = padded(dz_rows, (("seq", 0),), 2)
    dh_zero = dh_one
    for k in range(TAPS):
        dh_zero = dh_zero + contract_cols(dz_padded[4 - k : 4 - k + rows], conv_full[k])
    conv_term = jnp.stack([contract_rows(h_padded[k : k + rows], dz_rows) for k in range(TAPS)])
    embed_term = lax.dot_general(
        wide_hots[2 : 2 + rows].astype(jnp.float32),
        dh_zero,
        (((0,), (0,)), ((), ())),
        precision=lax.Precision.HIGHEST,
        preferred_element_type=jnp.float32,
    )
    grad_embed, grad_conv, grad_in, grad_out = reduced(conv_term, embed_term, in_term, out_term)
    return (output[None], grad_embed, grad_conv, grad_in, grad_out)


def solution(mesh):
    placed = (
        P(("dp", "sect"), "seq"),
        P(),
        P(None, "seq", None),
        P("seq", "sect"),
        P("sect", "seq"),
        P(("dp", "sect"), "seq", None),
    )
    return jax.shard_map(
        local,
        mesh=mesh,
        in_specs=placed,
        out_specs=(
            P(("dp", "sect"), "seq", None),
            P(None, None, "seq"),
            P(None, "seq", None),
            P("seq", "sect"),
            P("sect", "seq"),
        ),
        check_vma=False,
    )
```
